128 devices in a mesh: req: 8 (over x, core), pre: 16 (over y, z).
Axes of the slice: x: 4, y: 4, z: 4, core: 2. Of those that a mesh axis runs over, the one named last changes fastest.
Arguments:
- queries: bfloat16 [2048, 16384], P(('req', 'pre')), may hold values from -256 to 256
- prefix_ids: int32 [2048, 1], P(('req', 'pre')), may hold values from 0 to 15; in each aligned block of 16 rows (0 to 15, 16 to 31, ...) at most 2 rows name the same one
- suffix_lengths: int32 [2048], P(('req', 'pre')), may hold values from 1 to 256, as said below
- prefix_keys: bfloat16 [16, 4096, 1024], P('pre', 'req'), may hold values from -6 to 6
- prefix_values: bfloat16 [16, 4096, 1024], P('pre', 'req'), may hold values from -6 to 6
- suffix_keys: bfloat16 [2048, 256, 1024], P(('req', 'pre')), may hold values from -6 to 6
- suffix_values: bfloat16 [2048, 256, 1024], P(('req', 'pre')), may hold values from -6 to 6
Outputs:
- attended: bfloat16 [2048, 16384], P(('req', 'pre'))
The draws below stay inside these ranges and needn't reach their ends.
Inputs may be any that keep to these rules, and one draw needn't show every extreme that they name: `prefix_ids`: of the rows of one device, at most 2 name the same prefix; in every draw some device has exactly 2 rows naming one prefix. `suffix_lengths`: some request has exactly 256 suffix tokens.
All inputs are finite; a program needn't handle non-finite values.
Results may differ from the reference program's by a relative error of at most 0.022.
Values may be sent and summed in bfloat16 or wider, within the bound.
A program may use at most 256 MiB of HBM per device.

```python
import math
import jax
import jax.numpy as jnp
import numpy as np
from jax import lax

H = 128
KEY_VALUE_HEADS = 8
HEAD_SIZE = 128
PLEN = 4096
KEYS_DEV = 512
SUFFIX_TOKENS = 256
R_DEV = 16
CAP = 2
NPRE = 16
REQUESTS = 2048
N_REQ = 8


def draw_queries(key, part):
    key = jax.random.fold_in(key, 11)
    first = jax.random.fold_in(key, 0)
    base = jnp.clip(jax.random.normal(first, (REQUESTS, H * HEAD_SIZE), jnp.float32), -4.0, 4.0)
    return (base * 2.5).astype(jnp.bfloat16)


def draw_suffix_lengths(key, part):
    key = jax.random.fold_in(key, 23)
    lengths = jax.random.randint(key, (REQUESTS,), 1, SUFFIX_TOKENS + 1)
    return lengths.at[0].set(SUFFIX_TOKENS)


def block_levels(stream_key, extent, cuts, low, top_value):
    loudness = 1.0
    for dim, blocks in cuts:
        heights = jax.random.uniform(jax.random.fold_in(jax.random.fold_in(stream_key, 6), dim), (blocks,), jnp.float32, low / len(cuts), top_value / len(cuts))
        loudness = loudness * jnp.repeat(jnp.exp(heights), extent[dim] // blocks).reshape((-1,) + (1,) * (len(extent) - 1 - dim))
    return loudness


def deal_out(key, own, number, rows, amount, top, limit, lean):
    sequence = jax.random.permutation(key, amount)
    crowded, usual = shares(amount, rows * top, limit, lean, True), shares(amount, rows * top, limit, lean, False)
    places = jnp.arange(amount)

    def named(sizes, offset_by):
        used = int((sizes > 0).sum())
        fixed = max(1, used // 4)
        shifted = fixed + (places - fixed + offset_by * (used - fixed)) % max(1, amount - fixed)
        return jnp.zeros((amount,), jnp.int32).at[sequence[jnp.where(places < fixed, places, shifted)]].set(jnp.asarray(sizes, jnp.int32))

    sizes = jnp.where(number % 4 == 0, named(crowded, number // 4), named(usual, number - number // 4 - 1))
    mixed = jax.random.permutation(jax.random.fold_in(own, 3), amount)
    giver, receiver = mixed[0:amount // 2 * 2:2], mixed[1:amount // 2 * 2:2]
    margin = jnp.minimum(sizes[giver] - 1, limit - sizes[receiver]) // 2
    margin = jnp.where((giver == sequence[0]) | (receiver == sequence[0]) | (sizes[receiver] == 0), 0, jnp.maximum(margin, 0))
    shifted = jax.random.randint(jax.random.fold_in(own, 4), (amount // 2,), 0, 1 << 20) % (margin + 1)
    sizes = sizes.at[giver].add(-shifted).at[receiver].add(shifted)
    items = jnp.searchsorted(jnp.cumsum(sizes), jnp.arange(rows * top), side="right").astype(jnp.int32)
    listing = items.reshape(top, rows).T
    listing = listing[jax.random.permutation(jax.random.fold_in(own, 1), rows)]
    offset_by = jax.random.randint(jax.random.fold_in(own, 2), (rows, 1), 0, top)
    return jnp.take_along_axis(listing, (jnp.arange(top)[None, :] + offset_by) % top, axis=1)


def shares(count, total, limit, skew, full):
    weights = [(1 << 20) // math.isqrt(standing ** skew) + 1 for standing in range(1, count + 1)]
    largest = limit if full else min(limit, max(-(-total // count), total * weights[0] // sum(weights)))
    least = 1 if total - largest >= count - 1 else 0
    holding, rest = [largest] + [least] * (count - 1), total - largest - least * (count - 1)
    while rest > 0:
        candidates = [i for i in range(1, count) if holding[i] < largest] or [i for i in range(1, count) if holding[i] < limit]
        whole, remaining = sum([weights[i] for i in candidates]), rest
        for i in candidates:
            addition = min(limit - holding[i], max(1, remaining * weights[i] // whole), rest)
            holding[i] = holding[i] + addition
            rest = rest - addition
    return np.array(holding)


def noise(rng, extent, scale, limit, shards=(), dtype=jnp.bfloat16):
    result = scale * jax.random.normal(rng, extent, jnp.float32)
    if shards:
        result = result * block_levels(rng, extent, shards, -0.22, 0.18)
    return jnp.clip(result, -limit, limit).astype(dtype)


def setup_inputs(seed: int = 0) -> dict:
    streams_of = jax.random.split(jax.random.key(seed), 8)
    queries = draw_queries(jax.random.fold_in(streams_of[7], 71), 0)
    prefix_ids_keys = jax.random.split(jax.random.fold_in(streams_of[1], 1), REQUESTS // R_DEV)
    prefix_ids_turns = jax.random.permutation(jax.random.fold_in(streams_of[1], 3), REQUESTS // R_DEV)
    prefix_ids = jax.vmap(lambda own, number: deal_out(jax.random.fold_in(streams_of[1], 2), own, number, R_DEV, NPRE, 1, CAP, 2))(prefix_ids_keys, prefix_ids_turns).reshape((REQUESTS, 1))
    suffix_lengths = draw_suffix_lengths(jax.random.fold_in(streams_of[7], 71), 0)
    prefix_keys = noise(streams_of[3], (NPRE, PLEN, KEY_VALUE_HEADS * HEAD_SIZE), 1.0, 6.0, ((0, 16), (1, 8)))
    prefix_values = noise(streams_of[4], (NPRE, PLEN, KEY_VALUE_HEADS * HEAD_SIZE), 1.0, 6.0, ((0, 16), (1, 8)))
    suffix_keys = noise(streams_of[5], (REQUESTS, SUFFIX_TOKENS, KEY_VALUE_HEADS * HEAD_SIZE), 1.0, 6.0, ((0, 128),))
    suffix_values = noise(streams_of[6], (REQUESTS, SUFFIX_TOKENS, KEY_VALUE_HEADS * HEAD_SIZE), 1.0, 6.0, ((0, 128),))
    return dict(queries=queries, prefix_ids=prefix_ids, suffix_lengths=suffix_lengths, prefix_keys=prefix_keys, prefix_values=prefix_values, suffix_keys=suffix_keys, suffix_values=suffix_values)


def reference(queries, prefix_ids, suffix_lengths, prefix_keys, prefix_values, suffix_keys, suffix_values):
    score_scale = HEAD_SIZE ** -0.5
    group = H // KEY_VALUE_HEADS

    def one_request(items):
        query, wanted, length, request_keys, own_values = items
        grouped_queries = query.astype(jnp.float32).reshape(KEY_VALUE_HEADS, group, HEAD_SIZE)
        keys = lax.dynamic_index_in_dim(prefix_keys, wanted, 0, keepdims=False).astype(jnp.float32)
        keys = keys.reshape(N_REQ, KEYS_DEV, KEY_VALUE_HEADS, HEAD_SIZE)
        values = lax.dynamic_index_in_dim(prefix_values, wanted, 0, keepdims=False).astype(jnp.float32)
        values = values.reshape(N_REQ, KEYS_DEV, KEY_VALUE_HEADS, HEAD_SIZE)
        scores = jnp.einsum("gjd,bkgd->bgjk", grouped_queries, keys) * score_scale
        prefix_top = jnp.max(scores, axis=(0, 3))
        weights = jnp.exp(scores - prefix_top[None, :, :, None])
        block_den = lax.optimization_barrier(jnp.sum(weights, axis=-1).astype(jnp.bfloat16)).astype(jnp.float32)
        prefix_cast = lax.optimization_barrier(weights.astype(jnp.bfloat16)).astype(jnp.float32)
        block_num = jnp.einsum("bgjk,bkgd->bgjd", prefix_cast, values)
        block_num = lax.optimization_barrier(block_num.astype(jnp.bfloat16)).astype(jnp.float32)
        prefix_den = jnp.sum(block_den, axis=0)
        prefix_num = jnp.sum(block_num, axis=0)
        suffix_key_rows = request_keys.astype(jnp.float32).reshape(SUFFIX_TOKENS, KEY_VALUE_HEADS, HEAD_SIZE)
        svalues = own_values.astype(jnp.float32).reshape(SUFFIX_TOKENS, KEY_VALUE_HEADS, HEAD_SIZE)
        private_scores = jnp.einsum("zal,qzl->zaq", grouped_queries, suffix_key_rows) * score_scale
        valid = jnp.arange(SUFFIX_TOKENS) < length
        private_scores = jnp.where(valid, private_scores, -jnp.inf)
        suffix_top = jnp.max(private_scores, axis=-1)
        suffix_weights = jnp.where(valid, jnp.exp(private_scores - suffix_top[:, :, None]), 0.0)
        suffix_den = jnp.sum(suffix_weights, axis=-1)
        suffix_cast = lax.optimization_barrier(suffix_weights.astype(jnp.bfloat16)).astype(jnp.float32)
        suffix_num = jnp.einsum("gjs,sgd->gjd", suffix_cast, svalues)
        top = jnp.maximum(prefix_top, suffix_top)
        first = jnp.exp(prefix_top - top)
        second = jnp.exp(suffix_top - top)
        numer = prefix_num * first[:, :, None] + suffix_num * second[:, :, None]
        denom = prefix_den * first + suffix_den * second
        return (numer / denom[:, :, None]).reshape(H * HEAD_SIZE).astype(jnp.bfloat16)

    return lax.map(one_request, (queries, prefix_ids[:, 0], suffix_lengths, suffix_keys, suffix_values))
```

```python
import functools
import math

import jax
import jax.numpy as jnp
from jax import lax
from jax.experimental import pallas as pl
from jax.experimental.pallas import tpu as pltpu
from jax.sharding import PartitionSpec as P

HEAD_SIZE = 128
GROUP = 16
CAP = 2
MESH = pl.DeviceIdType.MESH
LOG2E = math.log2(math.e)
SCALE2 = HEAD_SIZE**-0.5 * LOG2E
NT = (((1,), (1,)), ((), ()))


def kernel(
    nr, npre, q_ref, meta_ref, len_ref, pk_ref, pv_ref, sk_ref, sv_ref, out_ref,
    mrecv, msm, qx, qo, qi, kb, vb, k2, v2, sk, sv, so, sl, oo, lo, ob, lb, ox, lx, of, lf,
    m_ss, m_rs, q_ss, q_rs, k_ss, k_rs, v_ss, v_rs, sk_s, sv_s, sm_s,
    y_ss, y_rs, o_ss, o_rs, l_ss, l_rs, f_ss, f_rs, g_ss, g_rs,
):
    rows = q_ref.shape[0]
    slots = nr * CAP
    positions = kb.shape[1]
    r = lax.axis_index("req")
    p = lax.axis_index("pre")

    def suffix_copies(i):
        return (
            pltpu.make_async_copy(sk_ref.at[i], sk.at[i], sk_s.at[i]),
            pltpu.make_async_copy(sv_ref.at[i], sv.at[i], sv_s.at[i]),
        )

    barrier = pltpu.get_barrier_semaphore()
    for k in range(1, nr):
        pl.semaphore_signal(barrier, inc=1, device_id=(lax.rem(r + k, nr), p), device_id_type=MESH)
    for k in range(1, npre):
        pl.semaphore_signal(barrier, inc=1, device_id=(r, lax.rem(p + k, npre)), device_id_type=MESH)

    def block(index, size):
        return pl.ds(pl.multiple_of(index * size, size), size)

    def x_copy(which, src, dst):
        if which == "meta":
            return meta_ref, mrecv.at[src], m_ss.at[dst], m_rs.at[src]
        if which == "query":
            return q_ref.at[:, block(dst, GROUP), :], qx.at[block(src, rows)], q_ss.at[dst], q_rs.at[src]
        if which == "key":
            return pk_ref.at[:, block(dst, HEAD_SIZE)], kb.at[src], k_ss.at[dst], k_rs.at[src]
        if which == "value":
            return pv_ref.at[:, block(dst, HEAD_SIZE)], vb.at[src], v_ss.at[dst], v_rs.at[src]
        if which == "result":
            return ox.at[block(dst, rows)], of.at[src], f_ss.at[dst], f_rs.at[src]
        return lx.at[block(dst, rows)], lf.at[src], g_ss.at[dst], g_rs.at[src]

    def y_copy(which, src, dst):
        if which == "query":
            return qo.at[block(dst, slots)], qi.at[block(src, slots)], y_ss.at[dst], y_rs.at[src]
        if which == "result":
            return oo.at[block(dst, slots)], ob.at[block(src, slots)], o_ss.at[dst], o_rs.at[src]
        return lo.at[block(dst, slots)], lb.at[block(src, slots)], l_ss.at[dst], l_rs.at[src]

    def x_remote(which, src, dst):
        a, b, c, d = x_copy(which, src, dst)
        return pltpu.make_async_remote_copy(a, b, c, d, device_id=(dst, p), device_id_type=MESH)

    def y_remote(which, src, dst):
        a, b, c, d = y_copy(which, src, dst)
        return pltpu.make_async_remote_copy(a, b, c, d, device_id=(r, dst), device_id_type=MESH)

    def x_own(which):
        a, b, _, d = x_copy(which, r, r)
        return pltpu.make_async_copy(a, b, d)

    def y_own(which):
        a, b, _, d = y_copy(which, p, p)
        return pltpu.make_async_copy(a, b, d)

    for which in ("meta", "query", "key", "value"):
        x_own(which).start()
    pl.semaphore_wait(barrier, nr - 1 + npre - 1)

    for which in ("meta", "query", "key", "value"):
        for k in range(1, nr):
            x_remote(which, r, lax.rem(r + k, nr)).start()

    @pl.loop(0, rows)
    def _(i):
        for copy in suffix_copies(i):
            copy.start()

    for which in ("meta", "query"):
        x_own(which).wait()
        for k in range(1, nr):
            x_remote(which, lax.rem(r + k, nr), r).wait_recv()
    to_smem = pltpu.make_async_copy(mrecv, msm, sm_s)
    to_smem.start()
    to_smem.wait()

    def place(dst):
        for src in range(nr):
            for rank in range(CAP):
                row = src * rows + msm[src, 0, dst * CAP + rank]
                qo[dst * slots + src * CAP + rank] = qx[row]

    @pl.loop(1, npre)
    def _(k):
        dst = lax.rem(p + k, npre)
        place(dst)
        y_remote("query", p, dst).start()

    place(p)
    y_own("query").start()

    heads = nr * GROUP
    tokens = sk.shape[1]
    lane = lax.broadcasted_iota(jnp.int32, (heads, tokens), 1)

    @pl.loop(0, rows)
    def _(i):
        for copy in suffix_copies(i):
            copy.wait()
        queries = q_ref[i]
        scores = jnp.concatenate(
            [
                lax.dot_general(
                    queries[g * GROUP : (g + 1) * GROUP],
                    sk[i, :, g * HEAD_SIZE : (g + 1) * HEAD_SIZE],
                    NT,
                    preferred_element_type=jnp.float32,
                )
                for g in range(nr)
            ],
            axis=0,
        )
        valid = lane < len_ref[i]
        scores = jnp.where(valid, scores * SCALE2, -jnp.inf)
        top = jnp.max(scores, axis=1, keepdims=True)
        weights = jnp.where(valid, jnp.exp2(scores - top), 0.0)
        den = jnp.sum(weights, axis=1, keepdims=True)
        cast = weights.astype(jnp.bfloat16)
        num = jnp.concatenate(
            [
                jnp.dot(
                    cast[g * GROUP : (g + 1) * GROUP],
                    sv[i, :, g * HEAD_SIZE : (g + 1) * HEAD_SIZE],
                    preferred_element_type=jnp.float32,
                )
                for g in range(nr)
            ],
            axis=0,
        )
        so[i] = num / den
        sl[i] = jnp.broadcast_to(top + jnp.log2(den), (heads, HEAD_SIZE))

    for which in ("key", "value"):
        x_own(which).wait()
        for k in range(1, nr):
            x_remote(which, lax.rem(r + k, nr), r).wait_recv()

    @pl.loop(0, nr)
    def _(b):
        span = block(b, positions)
        k2[span, :HEAD_SIZE] = kb[b]
        k2[span, HEAD_SIZE:] = kb[b]
        v2[span, :HEAD_SIZE] = vb[b]
        v2[span, HEAD_SIZE:] = jnp.ones((positions, HEAD_SIZE), jnp.bfloat16)

    tile = slots * GROUP
    picks = lax.broadcasted_iota(jnp.int32, (slots, GROUP, HEAD_SIZE), 1) == lax.broadcasted_iota(
        jnp.int32, (slots, GROUP, HEAD_SIZE), 2
    )

    def attend(src):
        scaled = qi[block(src, slots)].reshape(tile, HEAD_SIZE).astype(jnp.float32) * SCALE2
        high = scaled.astype(jnp.bfloat16)
        low = (scaled - high.astype(jnp.float32)).astype(jnp.bfloat16)
        scores = lax.dot_general(
            jnp.concatenate([high, low], axis=1), k2[...], NT, preferred_element_type=jnp.float32
        )
        top = jnp.max(scores, axis=1, keepdims=True)
        cast = jnp.exp2(scores - top).astype(jnp.bfloat16)
        both = jnp.dot(cast, v2[...], preferred_element_type=jnp.float32)
        den = both[:, HEAD_SIZE:]
        result = both[:, :HEAD_SIZE] / den
        level = top + jnp.log2(den)
        oo[block(src, slots)] = result.astype(jnp.bfloat16).reshape(slots, GROUP, HEAD_SIZE)
        lo[block(src, slots)] = jnp.sum(
            jnp.where(picks, level.reshape(slots, GROUP, HEAD_SIZE), 0.0), axis=1
        )

    @pl.loop(0, npre)
    def _(k):
        src = lax.rem(p + k, npre)

        @pl.when(k == 0)
        def _():
            y_own("query").wait()

        @pl.when(k > 0)
        def _():
            y_remote("query", src, p).wait_recv()

        attend(src)

        @pl.when(k == 0)
        def _():
            y_own("result").start()
            y_own("level").start()

        @pl.when(k > 0)
        def _():
            y_remote("result", p, src).start()
            y_remote("level", p, src).start()

    for which in ("result", "level"):
        y_own(which).wait()

        @pl.loop(1, npre)
        def _(k):
            y_remote(which, lax.rem(p + k, npre), p).wait_recv()

    def pick(dst):
        for i in range(rows):
            slot = msm[dst, 0, npre * CAP + i]
            ox[dst * rows + i] = ob[slot]
            lx[pl.ds(dst * rows + i, 1), :] = lb[pl.ds(slot, 1), :]

    @pl.loop(1, nr)
    def _(k):
        dst = lax.rem(r + k, nr)
        pick(dst)
        x_remote("result", r, dst).start()
        x_remote("level", r, dst).start()

    pick(r)
    x_own("result").start()
    x_own("level").start()
    for which in ("result", "level"):
        x_own(which).wait()
        for k in range(1, nr):
            x_remote(which, lax.rem(r + k, nr), r).wait_recv()

    chosen = lax.broadcasted_iota(jnp.int32, (nr, GROUP, HEAD_SIZE), 1) == lax.broadcasted_iota(
        jnp.int32, (nr, GROUP, HEAD_SIZE), 2
    )

    @pl.loop(0, rows)
    def _(i):
        spread = jnp.broadcast_to(lf[:, i, :][:, None, :], (nr, GROUP, HEAD_SIZE))
        first = jnp.sum(jnp.where(chosen, spread, 0.0), axis=2, keepdims=True)
        first = jnp.broadcast_to(first, (nr, GROUP, HEAD_SIZE)).reshape(heads, HEAD_SIZE)
        second = sl[i]
        top = jnp.maximum(first, second)
        first = jnp.exp2(first - top)
        second = jnp.exp2(second - top)
        prefix = of[:, i].astype(jnp.float32).reshape(heads, HEAD_SIZE)
        out_ref[i] = ((prefix * first + so[i] * second) / (first + second)).astype(jnp.bfloat16)

    for which in ("meta", "query", "key", "value", "result", "level"):
        for k in range(1, nr):
            x_remote(which, r, lax.rem(r + k, nr)).wait_send()
    for which in ("query", "result", "level"):

        @pl.loop(1, npre)
        def _(k):
            y_remote(which, p, lax.rem(p + k, npre)).wait_send()


def on_device(
    queries, prefix_ids, suffix_lengths, prefix_keys, prefix_values, suffix_keys, suffix_values
):
    rows, width = queries.shape
    npre = lax.axis_size("pre")
    nr = lax.axis_size("req")
    heads = nr * GROUP
    slots = nr * CAP
    positions = prefix_keys.shape[1]
    tokens = suffix_keys.shape[1]
    assert width == heads * HEAD_SIZE

    wanted = prefix_ids[:, 0]
    order = jnp.arange(rows)
    before = (order[None, :] < order[:, None]) & (wanted[None, :] == wanted[:, None])
    rank = jnp.sum(before.astype(jnp.int32), axis=1)
    named = wanted * CAP + rank
    holders = jnp.sum(
        jnp.where(jnp.arange(npre * CAP)[:, None] == named[None, :], order[None, :], 0), axis=1
    )
    places = wanted * slots + lax.axis_index("req") * CAP + rank
    meta = jnp.concatenate([holders, places]).astype(jnp.int32)
    meta = jnp.broadcast_to(jnp.pad(meta, (0, 128 - meta.shape[0]))[None, :], (8, 128))

    bf16, f32 = jnp.bfloat16, jnp.float32
    vmem = pl.BlockSpec(memory_space=pltpu.VMEM)
    smem = pl.BlockSpec(memory_space=pltpu.SMEM)
    hbm = pl.BlockSpec(memory_space=pl.ANY)
    dma = pltpu.SemaphoreType.DMA
    out = pl.pallas_call(
        functools.partial(kernel, nr, npre),
        out_shape=jax.ShapeDtypeStruct((rows, heads, HEAD_SIZE), bf16),
        in_specs=[vmem, vmem, smem, hbm, hbm, hbm, hbm],
        out_specs=vmem,
        scratch_shapes=[
            pltpu.VMEM((nr, 8, 128), jnp.int32),
            pltpu.SMEM((nr, 8, 128), jnp.int32),
            pltpu.VMEM((nr * rows, GROUP, HEAD_SIZE), bf16),
            pltpu.VMEM((npre * slots, GROUP, HEAD_SIZE), bf16),
            pltpu.VMEM((npre * slots, GROUP, HEAD_SIZE), bf16),
            pltpu.VMEM((nr, positions, HEAD_SIZE), bf16),
            pltpu.VMEM((nr, positions, HEAD_SIZE), bf16),
            pltpu.VMEM((nr * positions, 2 * HEAD_SIZE), bf16),
            pltpu.VMEM((nr * positions, 2 * HEAD_SIZE), bf16),
            pltpu.VMEM((rows, tokens, nr * HEAD_SIZE), bf16),
            pltpu.VMEM((rows, tokens, nr * HEAD_SIZE), bf16),
            pltpu.VMEM((rows, heads, HEAD_SIZE), f32),
            pltpu.VMEM((rows, heads, HEAD_SIZE), f32),
            pltpu.VMEM((npre * slots, GROUP, HEAD_SIZE), bf16),
            pltpu.VMEM((npre * slots, HEAD_SIZE), f32),
            pltpu.VMEM((npre * slots, GROUP, HEAD_SIZE), bf16),
            pltpu.VMEM((npre * slots, HEAD_SIZE), f32),
            pltpu.VMEM((nr * rows, GROUP, HEAD_SIZE), bf16),
            pltpu.VMEM((nr * rows, HEAD_SIZE), f32),
            pltpu.VMEM((nr, rows, GROUP, HEAD_SIZE), bf16),
            pltpu.VMEM((nr, rows, HEAD_SIZE), f32),
        ]
        + [dma((nr,))] * 8
        + [dma((rows,)), dma((rows,)), dma]
        + [dma((npre,))] * 6
        + [dma((nr,))] * 4,
        compiler_params=pltpu.CompilerParams(
            collective_id=0, has_side_effects=True, vmem_limit_bytes=60 * 1024 * 1024
        ),
    )(
        queries.reshape(rows, heads, HEAD_SIZE),
        meta,
        suffix_lengths,
        prefix_keys[0],
        prefix_values[0],
        suffix_keys,
        suffix_values,
    )
    return out.reshape(rows, width)


def solution(mesh):
    in_specs = (
        P(("req", "pre"), None),
        P(("req", "pre"), None),
        P(("req", "pre")),
        P("pre", "req", None),
        P("pre", "req", None),
        P(("req", "pre"), None, None),
        P(("req", "pre"), None, None),
    )
    out_specs = P(("req", "pre"), None)
    return jax.shard_map(
        on_device, mesh=mesh, in_specs=in_specs, out_specs=out_specs, check_vma=False
    )
```

```python
import functools
import math

import jax
import jax.numpy as jnp
from jax import lax
from jax.experimental import pallas as pl
from jax.experimental.pallas import tpu as pltpu
from jax.sharding import PartitionSpec as P

HEAD_SIZE = 128
GROUP = 16
CAP = 2
CORES = 2
CHUNK = 256
TILE = 512
ALONG_Z = 4
MESH = pl.DeviceIdType.MESH
LOG2E = math.log2(math.e)
SCALE2 = HEAD_SIZE**-0.5 * LOG2E
NT = (((1,), (1,)), ((), ()))


def kernel(
    nr, npre, q_ref, ids_ref, len_ref, pk_ref, pv_ref, sk_ref, sv_ref, out_ref,
    meta, mrecv, msm, qx_a, qx_b, qo, qi, kb, vb, kt, acc, high, skv, so, sl, oo, lo, ob_a, ob_b, lb_a, lb_b, ox, lx, of, lf, outv,
    m_ss, m_rs, m_os, q_ss, q_rs, q_os, k_ss, k_rs, v_ss, v_rs, km_ss, vm_ss, s_s, sm_s,
    y_ss, y_rs, y_os, o_ss, o_rs, o_os, l_ss, l_rs, l_os, f_ss, f_rs, f_os, g_ss, g_rs, g_os, out_s,
):
    qx, ob, lb = (qx_a, qx_b), (ob_a, ob_b), (lb_a, lb_b)
    rows = q_ref.shape[0]
    nx = nr // CORES
    slots = nx * CAP
    positions = kb.shape[2]
    heads = nr * GROUP
    tokens = skv.shape[2]
    r = lax.axis_index("req")
    p = lax.axis_index("pre")
    x = r // CORES
    core = lax.rem(r, CORES)
    mate = x * CORES + 1 - core

    tile = min(TILE, npre * slots * GROUP)
    sources = tile // (slots * GROUP)
    tiles = npre // sources
    tile_slots = sources * slots

    def block(index, size):
        return pl.ds(pl.multiple_of(index * size, size), size)

    def along(k):
        return lax.rem(x + k, nx)

    steps = [0, 1, nx - 1][:nx] + list(range(2, nx - 1))
    steps = list(dict.fromkeys(steps))

    def there(k):
        across = lax.rem(k, ALONG_Z)
        down = lax.rem(across + k // ALONG_Z, npre // ALONG_Z)
        return (
            lax.rem(p // ALONG_Z + down, npre // ALONG_Z) * ALONG_Z
            + lax.rem(lax.rem(p, ALONG_Z) + across, ALONG_Z)
        )

    def back(k):
        across = lax.rem(k, ALONG_Z)
        down = lax.rem(across + k // ALONG_Z, npre // ALONG_Z)
        return (
            lax.rem(p // ALONG_Z + npre // ALONG_Z - down, npre // ALONG_Z) * ALONG_Z
            + lax.rem(lax.rem(p, ALONG_Z) + ALONG_Z - across, ALONG_Z)
        )

    def suffix_copies(i):
        return (
            pltpu.make_async_copy(sk_ref.at[i], skv.at[i, 0], s_s.at[i]),
            pltpu.make_async_copy(sv_ref.at[i], skv.at[i, 1], s_s.at[i]),
        )

    def x_copy(which, h, src, dst, part=0):
        if which == "meta":
            return meta, mrecv.at[src], m_ss, m_rs, m_os
        if which == "query":
            head = dst * CORES + h
            return (
                q_ref.at[:, block(head, GROUP), :],
                qx[h].at[block(src, rows)],
                q_ss.at[h],
                q_rs.at[h],
                q_os.at[h],
            )
        if which == "key":
            return pk_ref.at[:, block(dst * CORES + h, HEAD_SIZE)], kb.at[h, part], k_ss.at[h], k_rs.at[h, part], k_rs.at[h, part]
        if which == "value":
            return (
                pv_ref.at[:, block(dst * CORES + h, HEAD_SIZE)],
                vb.at[h, part, :, pl.ds(0, HEAD_SIZE)],
                v_ss.at[h],
                v_rs.at[h, part],
                v_rs.at[h, part],
            )
        if which == "result":
            return ox.at[h, block(dst, rows)], of.at[h, src], f_ss.at[h], f_rs.at[h], f_os.at[h]
        return lx.at[h, block(dst, rows)], lf.at[h, src], g_ss.at[h], g_rs.at[h], g_os.at[h]

    def y_copy(which, h, k):
        at = block(k, slots)
        if which == "query":
            return qo.at[h, at], qi.at[h, at], y_ss.at[h], y_rs.at[h, k // sources], y_os.at[h], there(k)
        if which == "result":
            return oo.at[h, at], ob[h].at[at], o_ss.at[h], o_rs.at[h], o_os.at[h], back(k)
        return lo.at[h, at], lb[h].at[at], l_ss.at[h], l_rs.at[h], l_os.at[h], back(k)

    def x_remote(which, h, src, dst, part=0):
        a, b, c, d, _ = x_copy(which, h, src, dst, part)
        return pltpu.make_async_remote_copy(
            a, b, c, d, device_id=(dst * CORES + core, p), device_id_type=MESH
        )

    def y_remote(which, h, k):
        a, b, c, d, _, to = y_copy(which, h, k)
        return pltpu.make_async_remote_copy(a, b, c, d, device_id=(r, to), device_id_type=MESH)

    def sent(ref, sem):
        pltpu.make_async_remote_copy(
            ref, ref, sem, sem, device_id=(mate, p), device_id_type=MESH
        ).wait_send()

    def arrived(ref, sem):
        pltpu.make_async_remote_copy(
            ref, ref, sem, sem, device_id=(mate, p), device_id_type=MESH
        ).wait_recv()

    others = pl.ds(0, nx - 1)
    other_rows = pl.ds(0, (nx - 1) * rows)
    other_slots = pl.ds(slots, (npre - 1) * slots)

    def send_block(which, h, n):
        return x_remote(which, h, x, along(nx - steps[n]), CORES * n)

    def take_block(which, h, n):
        return x_remote(which, h, along(steps[n]), x, CORES * n)

    def x_own(which, h):
        a, b, _, _, d = x_copy(which, h, x, x)
        return pltpu.make_async_copy(a, b, d)

    def y_own(which, h):
        a, b, _, _, d, _ = y_copy(which, h, 0)
        return pltpu.make_async_copy(a, b, d)

    def mate_copy(which, h, n):
        mine, theirs = CORES * n, CORES * n + 1
        if which == "key":
            a, b = kb.at[h, mine], kb.at[h, theirs]
            first, c, d = pk_ref.at[:, block(x * CORES + h, HEAD_SIZE)], km_ss.at[h], k_rs.at[h, theirs]
        else:
            a, b = vb.at[h, mine, :, pl.ds(0, HEAD_SIZE)], vb.at[h, theirs, :, pl.ds(0, HEAD_SIZE)]
            first, c, d = pv_ref.at[:, block(x * CORES + h, HEAD_SIZE)], vm_ss.at[h], v_rs.at[h, theirs]
        return pltpu.make_async_remote_copy(
            first if n == 0 else a, b, c, d, device_id=(mate, p), device_id_type=MESH
        )

    vb[:, :, :, HEAD_SIZE:] = jnp.ones((CORES, nr, positions, HEAD_SIZE), jnp.bfloat16)
    barrier = pltpu.get_barrier_semaphore()
    pl.semaphore_signal(barrier, inc=1, device_id=(mate, p), device_id_type=MESH)
    for k in range(1, nx):
        pl.semaphore_signal(
            barrier, inc=1, device_id=(along(k) * CORES + core, p), device_id_type=MESH
        )
    for k in range(1, npre):
        pl.semaphore_signal(barrier, inc=1, device_id=(r, lax.rem(p + k, npre)), device_id_type=MESH)

    @pl.loop(0, rows)
    def _(i):
        for copy in suffix_copies(i):
            copy.start()

    for h in range(CORES):
        for which in ("query", "key", "value"):
            x_own(which, h).start()

    row = lax.broadcasted_iota(jnp.int32, (rows, HEAD_SIZE), 0)
    column = lax.broadcasted_iota(jnp.int32, (rows, HEAD_SIZE), 1)

    ids = jnp.zeros_like(row)
    other = jnp.zeros_like(row)
    for i in range(rows):
        ids = jnp.where(row == i, ids_ref[i], ids)
        other = jnp.where(column == i, ids_ref[i], other)

    def total(mask, values, axis):
        return jnp.sum(jnp.where(mask, values, 0), axis=axis, keepdims=True)

    named_before = (other == ids) & (column < row)
    rank = total(named_before, 1, 1)
    holders = total(ids * CAP + rank == column, row, 0)
    down = lax.rem(ids // ALONG_Z - p // ALONG_Z + npre, npre // ALONG_Z)
    across = lax.rem(lax.rem(ids, ALONG_Z) - lax.rem(p, ALONG_Z) + ALONG_Z, ALONG_Z)
    step = lax.rem(down - across + npre, npre // ALONG_Z) * ALONG_Z + across
    places = step * slots + x * CAP + jnp.minimum(rank, CAP - 1)
    places = total(column == npre * CAP + row, places, 0)
    meta[...] = jnp.broadcast_to(holders + places, meta.shape)
    x_own("meta", 0).start()

    lane = lax.broadcasted_iota(jnp.int32, (heads, tokens), 1)

    def suffix(i):
        pltpu.make_async_copy(skv.at[i], skv.at[i], s_s.at[i]).wait()
        queries = q_ref[i]
        scores = jnp.concatenate(
            [
                lax.dot_general(
                    queries[g * GROUP : (g + 1) * GROUP],
                    skv[i, 0, :, g * HEAD_SIZE : (g + 1) * HEAD_SIZE],
                    NT,
                    preferred_element_type=jnp.float32,
                )
                for g in range(nr)
            ],
            axis=0,
        )
        valid = lane < len_ref[i]
        scores = jnp.where(valid, scores * SCALE2, -jnp.inf)
        top = jnp.max(scores, axis=1, keepdims=True)
        weights = jnp.where(valid, jnp.exp2(scores - top), 0.0)
        den = jnp.sum(weights, axis=1, keepdims=True)
        cast = weights.astype(jnp.bfloat16)
        num = jnp.concatenate(
            [
                jnp.dot(
                    cast[g * GROUP : (g + 1) * GROUP],
                    skv[i, 1, :, g * HEAD_SIZE : (g + 1) * HEAD_SIZE],
                    preferred_element_type=jnp.float32,
                )
                for g in range(nr)
            ],
            axis=0,
        )
        so[i] = num / den
        sl[i] = jnp.broadcast_to(top + jnp.log2(den), (heads, HEAD_SIZE))

    early = rows // 2
    pl.loop(0, early)(suffix)

    pl.semaphore_wait(barrier, 1 + nx - 1 + npre - 1)
    for k in range(1, nx):
        x_remote("meta", 0, x, along(k)).start()
    for h in range(CORES):
        for k in range(1, nx):
            x_remote("query", h, x, along(k)).start()
    for h in range(CORES):
        for which in ("key", "value"):
            mate_copy(which, h, 0).start()
        for n in range(1, nx):
            for which in ("key", "value"):
                send_block(which, h, n).start()

    pl.loop(early, rows)(suffix)

    x_own("meta", 0).wait()
    arrived(mrecv.at[others], m_rs)
    to_smem = pltpu.make_async_copy(mrecv, msm, sm_s)
    to_smem.start()
    to_smem.wait()

    for h in range(CORES):
        x_own("query", h).wait()
        arrived(qx[h].at[other_rows], q_rs.at[h])

        def place(k, h=h):
            dst = there(k)
            for src in range(nx):
                for rank in range(CAP):
                    row = src * rows + jnp.clip(msm[src, 0, dst * CAP + rank], 0, rows - 1)
                    qo[h, k * slots + src * CAP + rank] = qx[h][row]

        @pl.loop(1, npre)
        def _(k, h=h, place=place):
            place(k)
            y_remote("query", h, k).start()

        place(0)
        y_own("query", h).start()

    picks = lax.broadcasted_iota(jnp.int32, (tile_slots, GROUP, HEAD_SIZE), 1) == lax.broadcasted_iota(
        jnp.int32, (tile_slots, GROUP, HEAD_SIZE), 2
    )

    chunk = min(CHUNK, positions)

    def attend(h, t, some):
        span = block(t, tile_slots)
        hold = block(t, tile)
        scaled = qi[h, span].reshape(tile, HEAD_SIZE).astype(jnp.float32) * SCALE2
        upper = scaled.astype(jnp.bfloat16)
        lower = (scaled - upper.astype(jnp.float32)).astype(jnp.bfloat16)
        queries = jnp.concatenate([upper, lower], axis=1)
        if 0 in some:
            top = jnp.full((tile, 1), -jnp.inf, jnp.float32)
            both = jnp.zeros((tile, 2 * HEAD_SIZE), jnp.float32)
        else:
            top = jnp.max(high[hold, :], axis=1, keepdims=True)
            both = acc[hold, :]
        for part in range(CORES * some[0], CORES * (some[-1] + 1)):
            for at in range(0, positions, chunk):
                scores = jnp.dot(
                    queries, kt[h, part, :, at : at + chunk], preferred_element_type=jnp.float32
                )
                higher = jnp.maximum(top, jnp.max(scores, axis=1, keepdims=True))
                cast = jnp.exp2(scores - higher).astype(jnp.bfloat16)
                both = both * jnp.exp2(top - higher) + jnp.dot(
                    cast, vb[h, part, at : at + chunk, :], preferred_element_type=jnp.float32
                )
                top = higher
        if nx - 1 not in some:
            high[hold, :] = jnp.broadcast_to(top, (tile, HEAD_SIZE))
            acc[hold, :] = both
            return
        den = both[:, HEAD_SIZE:]
        result = both[:, :HEAD_SIZE] / den
        level = top + jnp.log2(den)
        oo[h, span] = result.astype(jnp.bfloat16).reshape(tile_slots, GROUP, HEAD_SIZE)
        lo[h, span] = jnp.sum(
            jnp.where(picks, level.reshape(tile_slots, GROUP, HEAD_SIZE), 0.0), axis=1
        )

    def relay(h, some):
        for n in some:
            for which in ("key", "value"):
                if n > 0:
                    take_block(which, h, n).wait_recv()
                    mate_copy(which, h, n).start()

    def ready(h, some):
        for n in some:
            for which in ("key", "value"):
                if n == 0:
                    x_own(which, h).wait()
                mate_copy(which, h, n).wait_recv()

        @pl.loop(CORES * some[0], CORES * (some[-1] + 1))
        def _(part):
            turned = kb[h, part].T
            kt[h, part, :HEAD_SIZE] = turned
            kt[h, part, HEAD_SIZE:] = turned

    def prefix(h, some, after=None):
        @pl.loop(0, tiles)
        def _(t):
            if 0 in some:

                @pl.when(t == 0)
                def _():
                    y_own("query", h).wait()

                    arrived(qi.at[h, pl.ds(slots, tile_slots - slots)], y_rs.at[h, 0])

                @pl.when(t > 0)
                def _():
                    arrived(qi.at[h, block(t, tile_slots)], y_rs.at[h, t])

            attend(h, t, some)
            if nx - 1 in some:

                @pl.when(t == 0)
                def _():
                    y_own("result", h).start()
                    y_own("level", h).start()

                for s in range(sources):
                    k = t * sources + s

                    @pl.when(k > 0)
                    def _():
                        y_remote("result", h, k).start()
                        y_remote("level", h, k).start()

            if after is not None:
                pl.when(t == max(tiles - 2, 0))(after)

    def give_back(h):
        for which in ("result", "level"):
            y_own(which, h).wait()
        arrived(ob[h].at[other_slots], o_rs.at[h])
        arrived(lb[h].at[other_slots], l_rs.at[h])

        def pick(dst):
            for i in range(rows):
                slot = jnp.clip(msm[dst, 0, npre * CAP + i], 0, npre * slots - 1)
                ox[h, dst * rows + i] = ob[h][slot]
                lx[h, pl.ds(dst * rows + i, 1), :] = lb[h][pl.ds(slot, 1), :]

        for k in range(1, nx):
            dst = along(k)
            pick(dst)
            x_remote("result", h, x, dst).start()
            x_remote("level", h, x, dst).start()
        pick(x)
        x_own("result", h).start()
        x_own("level", h).start()

    chosen = lax.broadcasted_iota(jnp.int32, (nx, GROUP, HEAD_SIZE), 1) == lax.broadcasted_iota(
        jnp.int32, (nx, GROUP, HEAD_SIZE), 2
    )

    def combine(h):
        for which in ("result", "level"):
            x_own(which, h).wait()
        arrived(of.at[h, others], f_rs.at[h])
        arrived(lf.at[h, others], g_rs.at[h])

        @pl.loop(0, rows)
        def _(i):
            spread = jnp.broadcast_to(lf[h, :, i, :][:, None, :], (nx, GROUP, HEAD_SIZE))
            levels = jnp.sum(jnp.where(chosen, spread, 0.0), axis=2, keepdims=True)
            for g in range(nx):
                mine = slice((g * CORES + h) * GROUP, (g * CORES + h + 1) * GROUP)
                first = jnp.broadcast_to(levels[g], (GROUP, HEAD_SIZE))
                second = sl[i, mine]
                top = jnp.maximum(first, second)
                first = jnp.exp2(first - top)
                second = jnp.exp2(second - top)
                outv[i, mine] = (
                    (of[h, g, i].astype(jnp.float32) * first + so[i, mine] * second)
                    / (first + second)
                ).astype(jnp.bfloat16)
            if h == CORES - 1:
                pltpu.make_async_copy(outv.at[i], out_ref.at[i], out_s).start()

    near, far = [0], list(range(1, nx))
    ready(0, near)
    prefix(0, near)
    relay(0, far)
    ready(0, far)
    prefix(0, far)
    ready(1, near)
    prefix(1, near, lambda: relay(1, far))
    ready(1, far)
    prefix(1, far, lambda: give_back(0))

    sent(mrecv.at[others], m_ss)
    for h in range(CORES):
        sent(qx[h].at[other_rows], q_ss.at[h])
        sent(kb.at[h, others], k_ss.at[h])
        sent(vb.at[h, others, :, pl.ds(0, HEAD_SIZE)], v_ss.at[h])
        sent(kb.at[h, pl.ds(0, nx)], km_ss.at[h])
        sent(vb.at[h, pl.ds(0, nx), :, pl.ds(0, HEAD_SIZE)], vm_ss.at[h])
        sent(qo.at[h, other_slots], y_ss.at[h])
    combine(0)
    give_back(1)
    for h in range(CORES):
        sent(oo.at[h, other_slots], o_ss.at[h])
        sent(lo.at[h, other_slots], l_ss.at[h])
    combine(1)
    for h in range(CORES):
        sent(ox.at[h, other_rows], f_ss.at[h])
        sent(lx.at[h, other_rows], g_ss.at[h])
    pltpu.make_async_copy(outv, out_ref, out_s).wait()


def on_device(
    queries, prefix_ids, suffix_lengths, prefix_keys, prefix_values, suffix_keys, suffix_values
):
    rows, width = queries.shape
    npre = lax.axis_size("pre")
    nr = lax.axis_size("req")
    nx = nr // CORES
    heads = nr * GROUP
    slots = nx * CAP
    positions = prefix_keys.shape[1]
    tokens = suffix_keys.shape[1]
    assert width == heads * HEAD_SIZE

    bf16, f32 = jnp.bfloat16, jnp.float32
    vmem = pl.BlockSpec(memory_space=pltpu.VMEM)
    smem = pl.BlockSpec(memory_space=pltpu.SMEM)
    hbm = pl.BlockSpec(memory_space=pl.ANY)
    dma = pltpu.SemaphoreType.DMA
    moved = pltpu.VMEM((CORES, npre * slots, GROUP, HEAD_SIZE), bf16)
    levels = pltpu.VMEM((CORES, npre * slots, HEAD_SIZE), f32)
    out = pl.pallas_call(
        functools.partial(kernel, nr, npre),
        out_shape=jax.ShapeDtypeStruct((rows, heads, HEAD_SIZE), bf16),
        in_specs=[vmem, smem, smem, hbm, hbm, hbm, hbm],
        out_specs=hbm,
        scratch_shapes=[
            pltpu.VMEM((8, 128), jnp.int32),
            pltpu.VMEM((nx, 8, 128), jnp.int32),
            pltpu.SMEM((nx, 8, 128), jnp.int32),
            pltpu.VMEM((nx * rows, GROUP, HEAD_SIZE), bf16),
            pltpu.VMEM((nx * rows, GROUP, HEAD_SIZE), bf16),
            moved,
            moved,
            pltpu.VMEM((CORES, nr, positions, HEAD_SIZE), bf16),
            pltpu.VMEM((CORES, nr, positions, 2 * HEAD_SIZE), bf16),
            pltpu.VMEM((CORES, nr, 2 * HEAD_SIZE, positions), bf16),
            pltpu.VMEM((npre * slots * GROUP, 2 * HEAD_SIZE), f32),
            pltpu.VMEM((npre * slots * GROUP, HEAD_SIZE), f32),
            pltpu.VMEM((rows, 2, tokens, nr * HEAD_SIZE), bf16),
            pltpu.VMEM((rows, heads, HEAD_SIZE), f32),
            pltpu.VMEM((rows, heads, HEAD_SIZE), f32),
            moved,
            levels,
            pltpu.VMEM((npre * slots, GROUP, HEAD_SIZE), bf16),
            pltpu.VMEM((npre * slots, GROUP, HEAD_SIZE), bf16),
            pltpu.VMEM((npre * slots, HEAD_SIZE), f32),
            pltpu.VMEM((npre * slots, HEAD_SIZE), f32),
            pltpu.VMEM((CORES, nx * rows, GROUP, HEAD_SIZE), bf16),
            pltpu.VMEM((CORES, nx * rows, HEAD_SIZE), f32),
            pltpu.VMEM((CORES, nx, rows, GROUP, HEAD_SIZE), bf16),
            pltpu.VMEM((CORES, nx, rows, HEAD_SIZE), f32),
            pltpu.VMEM((rows, heads, HEAD_SIZE), bf16),
        ]
        + [dma] * 3
        + [dma((CORES,))] * 3
        + [dma((CORES,)), dma((CORES, nr))] * 2
        + [dma((CORES,))] * 2
        + [dma((rows,)), dma]
        + [dma((CORES,)), dma((CORES, npre * slots * GROUP // TILE + 1)), dma((CORES,))]
        + [dma((CORES,))] * 12
        + [dma],
        compiler_params=pltpu.CompilerParams(
            collective_id=0, has_side_effects=True, vmem_limit_bytes=60 * 1024 * 1024
        ),
    )(
        queries.reshape(rows, heads, HEAD_SIZE),
        prefix_ids[:, 0],
        suffix_lengths,
        prefix_keys[0],
        prefix_values[0],
        suffix_keys,
        suffix_values,
    )
    return out.reshape(rows, width)


def solution(mesh):
    in_specs = (
        P(("req", "pre"), None),
        P(("req", "pre"), None),
        P(("req", "pre")),
        P("pre", "req", None),
        P("pre", "req", None),
        P(("req", "pre"), None, None),
        P(("req", "pre"), None, None),
    )
    out_specs = P(("req", "pre"), None)
    return jax.shard_map(
        on_device, mesh=mesh, in_specs=in_specs, out_specs=out_specs, check_vma=False
    )
```

```python
import functools
import math

import jax
import jax.numpy as jnp
from jax import lax
from jax.experimental import pallas as pl
from jax.experimental.pallas import tpu as pltpu
from jax.sharding import PartitionSpec as P

HEAD_SIZE = 128
GROUP = 16
CAP = 2
CORES = 2
CHUNK = 256
TILE = 512
ALONG_Z = 4
MESH = pl.DeviceIdType.MESH
LOG2E = math.log2(math.e)
SCALE2 = HEAD_SIZE**-0.5 * LOG2E
NT = (((1,), (1,)), ((), ()))


def kernel(
    nr, npre, flat_ref, ids_ref, len_ref, pk_ref, pv_ref, sk_ref, sv_ref, out_ref,
    q_ref, meta, mrecv, msm, qx_a, qx_b, qo, qi, kb, vb, kt, acc, high, skv, so, sl, oo, lo, ob_a, ob_b, lb_a, lb_b, ox, lx, of, lf, outv, flat,
    m_ss, m_rs, m_os, q_ss, q_rs, q_os, k_ss, k_rs, v_ss, v_rs, km_ss, vm_ss, s_s, sm_s,
    y_ss, y_rs, y_os, o_ss, o_rs, o_os, l_ss, l_rs, l_os, f_ss, f_rs, f_os, g_ss, g_rs, g_os, out_s,
):
    qx, ob, lb = (qx_a, qx_b), (ob_a, ob_b), (lb_a, lb_b)
    rows = flat_ref.shape[0]
    nx = nr // CORES
    slots = nx * CAP
    positions = kb.shape[2]
    heads = nr * GROUP
    tokens = skv.shape[2]
    r = lax.axis_index("req")
    p = lax.axis_index("pre")
    x = r // CORES
    core = lax.rem(r, CORES)
    mate = x * CORES + 1 - core

    tile = min(TILE, npre * slots * GROUP)
    sources = tile // (slots * GROUP)
    tiles = npre // sources
    tile_slots = sources * slots

    def block(index, size):
        return pl.ds(pl.multiple_of(index * size, size), size)

    def along(k):
        return lax.rem(x + k, nx)

    steps = [0, 1, nx - 1][:nx] + list(range(2, nx - 1))
    steps = list(dict.fromkeys(steps))

    def there(k):
        across = lax.rem(k, ALONG_Z)
        down = lax.rem(across + k // ALONG_Z, npre // ALONG_Z)
        return (
            lax.rem(p // ALONG_Z + down, npre // ALONG_Z) * ALONG_Z
            + lax.rem(lax.rem(p, ALONG_Z) + across, ALONG_Z)
        )

    def back(k):
        across = lax.rem(k, ALONG_Z)
        down = lax.rem(across + k // ALONG_Z, npre // ALONG_Z)
        return (
            lax.rem(p // ALONG_Z + npre // ALONG_Z - down, npre // ALONG_Z) * ALONG_Z
            + lax.rem(lax.rem(p, ALONG_Z) + ALONG_Z - across, ALONG_Z)
        )

    def suffix_copies(i):
        return (
            pltpu.make_async_copy(sk_ref.at[i], skv.at[i, 0], s_s.at[i]),
            pltpu.make_async_copy(sv_ref.at[i], skv.at[i, 1], s_s.at[i]),
        )

    def x_copy(which, h, src, dst, part=0):
        if which == "meta":
            return meta, mrecv.at[src], m_ss, m_rs, m_os
        if which == "query":
            head = dst * CORES + h
            return (
                q_ref.at[:, block(head, GROUP), :],
                qx[h].at[block(src, rows)],
                q_ss.at[h],
                q_rs.at[h],
                q_os.at[h],
            )
        if which == "key":
            return pk_ref.at[:, block(dst * CORES + h, HEAD_SIZE)], kb.at[h, part], k_ss.at[h], k_rs.at[h, part], k_rs.at[h, part]
        if which == "value":
            return (
                pv_ref.at[:, block(dst * CORES + h, HEAD_SIZE)],
                vb.at[h, part, :, pl.ds(0, HEAD_SIZE)],
                v_ss.at[h],
                v_rs.at[h, part],
                v_rs.at[h, part],
            )
        if which == "result":
            return ox.at[h, block(dst, rows)], of.at[h, src], f_ss.at[h], f_rs.at[h], f_os.at[h]
        return lx.at[h, block(dst, rows)], lf.at[h, src], g_ss.at[h], g_rs.at[h], g_os.at[h]

    def y_copy(which, h, k):
        at = block(k, slots)
        if which == "query":
            return qo.at[h, at], qi.at[h, at], y_ss.at[h], y_rs.at[h, k // sources], y_os.at[h], there(k)
        if which == "result":
            return oo.at[h, at], ob[h].at[at], o_ss.at[h], o_rs.at[h], o_os.at[h], back(k)
        return lo.at[h, at], lb[h].at[at], l_ss.at[h], l_rs.at[h], l_os.at[h], back(k)

    def x_remote(which, h, src, dst, part=0):
        a, b, c, d, _ = x_copy(which, h, src, dst, part)
        return pltpu.make_async_remote_copy(
            a, b, c, d, device_id=(dst * CORES + core, p), device_id_type=MESH
        )

    def y_remote(which, h, k):
        a, b, c, d, _, to = y_copy(which, h, k)
        return pltpu.make_async_remote_copy(a, b, c, d, device_id=(r, to), device_id_type=MESH)

    def sent(ref, sem):
        pltpu.make_async_remote_copy(
            ref, ref, sem, sem, device_id=(mate, p), device_id_type=MESH
        ).wait_send()

    def arrived(ref, sem):
        pltpu.make_async_remote_copy(
            ref, ref, sem, sem, device_id=(mate, p), device_id_type=MESH
        ).wait_recv()

    others = pl.ds(0, nx - 1)
    other_rows = pl.ds(0, (nx - 1) * rows)
    other_slots = pl.ds(slots, (npre - 1) * slots)

    def send_block(which, h, n):
        return x_remote(which, h, x, along(nx - steps[n]), CORES * n)

    def take_block(which, h, n):
        return x_remote(which, h, along(steps[n]), x, CORES * n)

    def x_own(which, h):
        a, b, _, _, d = x_copy(which, h, x, x)
        return pltpu.make_async_copy(a, b, d)

    def y_own(which, h):
        a, b, _, _, d, _ = y_copy(which, h, 0)
        return pltpu.make_async_copy(a, b, d)

    def mate_copy(which, h, n):
        mine, theirs = CORES * n, CORES * n + 1
        if which == "key":
            a, b = kb.at[h, mine], kb.at[h, theirs]
            first, c, d = pk_ref.at[:, block(x * CORES + h, HEAD_SIZE)], km_ss.at[h], k_rs.at[h, theirs]
        else:
            a, b = vb.at[h, mine, :, pl.ds(0, HEAD_SIZE)], vb.at[h, theirs, :, pl.ds(0, HEAD_SIZE)]
            first, c, d = pv_ref.at[:, block(x * CORES + h, HEAD_SIZE)], vm_ss.at[h], v_rs.at[h, theirs]
        return pltpu.make_async_remote_copy(
            first if n == 0 else a, b, c, d, device_id=(mate, p), device_id_type=MESH
        )

    barrier = pltpu.get_barrier_semaphore()
    pl.semaphore_signal(barrier, inc=1, device_id=(mate, p), device_id_type=MESH)
    for k in range(1, nx):
        pl.semaphore_signal(
            barrier, inc=1, device_id=(along(k) * CORES + core, p), device_id_type=MESH
        )
    for k in range(1, npre):
        pl.semaphore_signal(barrier, inc=1, device_id=(r, lax.rem(p + k, npre)), device_id_type=MESH)

    vb[:, :, :, HEAD_SIZE:] = jnp.ones((CORES, nr, positions, HEAD_SIZE), jnp.bfloat16)
    wide = GROUP * HEAD_SIZE
    for g in range(nr):
        q_ref[:, g * GROUP : (g + 1) * GROUP, :] = flat_ref[:, g * wide : (g + 1) * wide].reshape(
            rows, GROUP, HEAD_SIZE
        )
    for h in range(CORES):
        for which in ("query", "key", "value"):
            x_own(which, h).start()

    row = lax.broadcasted_iota(jnp.int32, (rows, HEAD_SIZE), 0)
    column = lax.broadcasted_iota(jnp.int32, (rows, HEAD_SIZE), 1)

    ids = jnp.zeros_like(row)
    other = jnp.zeros_like(row)
    for i in range(rows):
        ids = jnp.where(row == i, ids_ref[i], ids)
        other = jnp.where(column == i, ids_ref[i], other)

    def total(mask, values, axis):
        return jnp.sum(jnp.where(mask, values, 0), axis=axis, keepdims=True)

    named_before = (other == ids) & (column < row)
    rank = total(named_before, 1, 1)
    holders = total(ids * CAP + rank == column, row, 0)
    down = lax.rem(ids // ALONG_Z - p // ALONG_Z + npre, npre // ALONG_Z)
    across = lax.rem(lax.rem(ids, ALONG_Z) - lax.rem(p, ALONG_Z) + ALONG_Z, ALONG_Z)
    step = lax.rem(down - across + npre, npre // ALONG_Z) * ALONG_Z + across
    places = step * slots + x * CAP + jnp.minimum(rank, CAP - 1)
    places = total(column == npre * CAP + row, places, 0)
    meta[...] = jnp.broadcast_to(holders + places, meta.shape)
    x_own("meta", 0).start()

    lane = lax.broadcasted_iota(jnp.int32, (heads, tokens), 1)

    def suffix(i):
        pltpu.make_async_copy(skv.at[i], skv.at[i], s_s.at[i]).wait()
        queries = q_ref[i]
        scores = jnp.concatenate(
            [
                lax.dot_general(
                    queries[g * GROUP : (g + 1) * GROUP],
                    skv[i, 0, :, g * HEAD_SIZE : (g + 1) * HEAD_SIZE],
                    NT,
                    preferred_element_type=jnp.float32,
                )
                for g in range(nr)
            ],
            axis=0,
        )
        valid = lane < len_ref[i]
        scores = jnp.where(valid, scores * SCALE2, -jnp.inf)
        top = jnp.max(scores, axis=1, keepdims=True)
        weights = jnp.where(valid, jnp.exp2(scores - top), 0.0)
        den = jnp.sum(weights, axis=1, keepdims=True)
        cast = weights.astype(jnp.bfloat16)
        num = jnp.concatenate(
            [
                jnp.dot(
                    cast[g * GROUP : (g + 1) * GROUP],
                    skv[i, 1, :, g * HEAD_SIZE : (g + 1) * HEAD_SIZE],
                    preferred_element_type=jnp.float32,
                )
                for g in range(nr)
            ],
            axis=0,
        )
        so[i] = num / den
        sl[i] = jnp.broadcast_to(top + jnp.log2(den), (heads, HEAD_SIZE))

    pl.semaphore_wait(barrier, 1 + nx - 1 + npre - 1)
    for k in range(1, nx):
        x_remote("meta", 0, x, along(k)).start()
    for h in range(CORES):
        for k in range(1, nx):
            x_remote("query", h, x, along(k)).start()
    for h in range(CORES):
        for which in ("key", "value"):
            mate_copy(which, h, 0).start()
        for n in range(1, nx):
            for which in ("key", "value"):
                send_block(which, h, n).start()

    @pl.loop(0, rows)
    def _(i):
        for copy in suffix_copies(i):
            copy.start()

    early = rows * 5 // 8
    pl.loop(0, early)(suffix)

    x_own("meta", 0).wait()
    arrived(mrecv.at[others], m_rs)
    to_smem = pltpu.make_async_copy(mrecv, msm, sm_s)
    to_smem.start()
    to_smem.wait()

    for h in range(CORES):
        x_own("query", h).wait()
        arrived(qx[h].at[other_rows], q_rs.at[h])

        def place(k, h=h):
            dst = there(k)
            for src in range(nx):
                for rank in range(CAP):
                    row = src * rows + jnp.clip(msm[src, 0, dst * CAP + rank], 0, rows - 1)
                    qo[h, k * slots + src * CAP + rank] = qx[h][row]

        @pl.loop(1, npre)
        def _(k, h=h, place=place):
            place(k)
            y_remote("query", h, k).start()

        place(0)
        y_own("query", h).start()

    pl.loop(early, rows)(suffix)

    picks = lax.broadcasted_iota(jnp.int32, (tile_slots, GROUP, HEAD_SIZE), 1) == lax.broadcasted_iota(
        jnp.int32, (tile_slots, GROUP, HEAD_SIZE), 2
    )

    chunk = min(CHUNK, positions)

    def attend(h, t, some):
        span = block(t, tile_slots)
        hold = block(t, tile)
        scaled = qi[h, span].reshape(tile, HEAD_SIZE).astype(jnp.float32) * SCALE2
        upper = scaled.astype(jnp.bfloat16)
        lower = (scaled - upper.astype(jnp.float32)).astype(jnp.bfloat16)
        queries = jnp.concatenate([upper, lower], axis=1)
        if 0 in some:
            top = jnp.full((tile, 1), -jnp.inf, jnp.float32)
            both = jnp.zeros((tile, 2 * HEAD_SIZE), jnp.float32)
        else:
            top = jnp.max(high[hold, :], axis=1, keepdims=True)
            both = acc[hold, :]
        for part in range(CORES * some[0], CORES * (some[-1] + 1)):
            for at in range(0, positions, chunk):
                scores = jnp.dot(
                    queries, kt[h, part, :, at : at + chunk], preferred_element_type=jnp.float32
                )
                higher = jnp.maximum(top, jnp.max(scores, axis=1, keepdims=True))
                cast = jnp.exp2(scores - higher).astype(jnp.bfloat16)
                both = both * jnp.exp2(top - higher) + jnp.dot(
                    cast, vb[h, part, at : at + chunk, :], preferred_element_type=jnp.float32
                )
                top = higher
        if nx - 1 not in some:
            high[hold, :] = jnp.broadcast_to(top, (tile, HEAD_SIZE))
            acc[hold, :] = both
            return
        den = both[:, HEAD_SIZE:]
        result = both[:, :HEAD_SIZE] / den
        level = top + jnp.log2(den)
        oo[h, span] = result.astype(jnp.bfloat16).reshape(tile_slots, GROUP, HEAD_SIZE)
        lo[h, span] = jnp.sum(
            jnp.where(picks, level.reshape(tile_slots, GROUP, HEAD_SIZE), 0.0), axis=1
        )

    def relay(h, some):
        for n in some:
            for which in ("key", "value"):
                if n > 0:
                    take_block(which, h, n).wait_recv()
                    mate_copy(which, h, n).start()

    def ready(h, some):
        for n in some:
            for which in ("key", "value"):
                if n == 0:
                    x_own(which, h).wait()
                mate_copy(which, h, n).wait_recv()

        @pl.loop(CORES * some[0], CORES * (some[-1] + 1))
        def _(part):
            turned = kb[h, part].T
            kt[h, part, :HEAD_SIZE] = turned
            kt[h, part, HEAD_SIZE:] = turned

    def prefix(h, some, after=None, when=max(tiles - 2, 0)):
        @pl.loop(0, tiles)
        def _(t):
            if 0 in some:

                @pl.when(t == 0)
                def _():
                    y_own("query", h).wait()

                    arrived(qi.at[h, pl.ds(slots, tile_slots - slots)], y_rs.at[h, 0])

                @pl.when(t > 0)
                def _():
                    arrived(qi.at[h, block(t, tile_slots)], y_rs.at[h, t])

            attend(h, t, some)
            if nx - 1 in some:

                @pl.when(t == 0)
                def _():
                    y_own("result", h).start()
                    y_own("level", h).start()

                for s in range(sources):
                    k = t * sources + s

                    @pl.when(k > 0)
                    def _():
                        y_remote("result", h, k).start()
                        y_remote("level", h, k).start()

            if after is not None:
                pl.when(t == when)(after)

    def give_back(h):
        for which in ("result", "level"):
            y_own(which, h).wait()
        arrived(ob[h].at[other_slots], o_rs.at[h])
        arrived(lb[h].at[other_slots], l_rs.at[h])

        def pick(dst):
            for i in range(rows):
                slot = jnp.clip(msm[dst, 0, npre * CAP + i], 0, npre * slots - 1)
                ox[h, dst * rows + i] = ob[h][slot]
                lx[h, pl.ds(dst * rows + i, 1), :] = lb[h][pl.ds(slot, 1), :]

        for k in range(1, nx):
            dst = along(k)
            pick(dst)
            x_remote("result", h, x, dst).start()
            x_remote("level", h, x, dst).start()
        pick(x)
        x_own("result", h).start()
        x_own("level", h).start()

    chosen = lax.broadcasted_iota(jnp.int32, (nx, GROUP, HEAD_SIZE), 1) == lax.broadcasted_iota(
        jnp.int32, (nx, GROUP, HEAD_SIZE), 2
    )

    def combine(h):
        for which in ("result", "level"):
            x_own(which, h).wait()
        arrived(of.at[h, others], f_rs.at[h])
        arrived(lf.at[h, others], g_rs.at[h])

        @pl.loop(0, rows)
        def _(i):
            spread = jnp.broadcast_to(lf[h, :, i, :][:, None, :], (nx, GROUP, HEAD_SIZE))
            levels = jnp.sum(jnp.where(chosen, spread, 0.0), axis=2, keepdims=True)
            for g in range(nx):
                mine = slice((g * CORES + h) * GROUP, (g * CORES + h + 1) * GROUP)
                first = jnp.broadcast_to(levels[g], (GROUP, HEAD_SIZE))
                second = sl[i, mine]
                top = jnp.maximum(first, second)
                first = jnp.exp2(first - top)
                second = jnp.exp2(second - top)
                outv[i, mine] = (
                    (of[h, g, i].astype(jnp.float32) * first + so[i, mine] * second)
                    / (first + second)
                ).astype(jnp.bfloat16)

        for g in range(h, nr, CORES):
            columns = pl.ds(g * wide, wide)
            flat[:, columns] = outv[:, g * GROUP : (g + 1) * GROUP, :].reshape(rows, wide)
            pltpu.make_async_copy(flat.at[:, columns], out_ref.at[:, columns], out_s).start()

    near, far = [0], list(range(1, nx))
    ready(0, near)
    prefix(0, near)
    relay(0, far)
    ready(0, far)
    prefix(0, far)
    ready(1, near)
    prefix(1, near, lambda: relay(1, far))
    ready(1, far)
    prefix(1, far, lambda: give_back(0), 0)

    sent(mrecv.at[others], m_ss)
    for h in range(CORES):
        sent(qx[h].at[other_rows], q_ss.at[h])
        sent(kb.at[h, others], k_ss.at[h])
        sent(vb.at[h, others, :, pl.ds(0, HEAD_SIZE)], v_ss.at[h])
        sent(kb.at[h, pl.ds(0, nx)], km_ss.at[h])
        sent(vb.at[h, pl.ds(0, nx), :, pl.ds(0, HEAD_SIZE)], vm_ss.at[h])
        sent(qo.at[h, other_slots], y_ss.at[h])
    combine(0)
    give_back(1)
    for h in range(CORES):
        sent(oo.at[h, other_slots], o_ss.at[h])
        sent(lo.at[h, other_slots], l_ss.at[h])
    combine(1)
    for h in range(CORES):
        sent(ox.at[h, other_rows], f_ss.at[h])
        sent(lx.at[h, other_rows], g_ss.at[h])
    pltpu.make_async_copy(flat, out_ref, out_s).wait()


def on_device(
    queries, prefix_ids, suffix_lengths, prefix_keys, prefix_values, suffix_keys, suffix_values
):
    rows, width = queries.shape
    npre = lax.axis_size("pre")
    nr = lax.axis_size("req")
    nx = nr // CORES
    heads = nr * GROUP
    slots = nx * CAP
    positions = prefix_keys.shape[1]
    tokens = suffix_keys.shape[1]
    assert width == heads * HEAD_SIZE

    bf16, f32 = jnp.bfloat16, jnp.float32
    vmem = pl.BlockSpec(memory_space=pltpu.VMEM)
    smem = pl.BlockSpec(memory_space=pltpu.SMEM)
    hbm = pl.BlockSpec(memory_space=pl.ANY)
    dma = pltpu.SemaphoreType.DMA
    moved = pltpu.VMEM((CORES, npre * slots, GROUP, HEAD_SIZE), bf16)
    levels = pltpu.VMEM((CORES, npre * slots, HEAD_SIZE), f32)
    out = pl.pallas_call(
        functools.partial(kernel, nr, npre),
        out_shape=jax.ShapeDtypeStruct((rows, width), bf16),
        in_specs=[vmem, smem, smem, hbm, hbm, hbm, hbm],
        out_specs=hbm,
        scratch_shapes=[
            pltpu.VMEM((rows, heads, HEAD_SIZE), bf16),
            pltpu.VMEM((8, 128), jnp.int32),
            pltpu.VMEM((nx, 8, 128), jnp.int32),
            pltpu.SMEM((nx, 8, 128), jnp.int32),
            pltpu.VMEM((nx * rows, GROUP, HEAD_SIZE), bf16),
            pltpu.VMEM((nx * rows, GROUP, HEAD_SIZE), bf16),
            moved,
            moved,
            pltpu.VMEM((CORES, nr, positions, HEAD_SIZE), bf16),
            pltpu.VMEM((CORES, nr, positions, 2 * HEAD_SIZE), bf16),
            pltpu.VMEM((CORES, nr, 2 * HEAD_SIZE, positions), bf16),
            pltpu.VMEM((npre * slots * GROUP, 2 * HEAD_SIZE), f32),
            pltpu.VMEM((npre * slots * GROUP, HEAD_SIZE), f32),
            pltpu.VMEM((rows, 2, tokens, nr * HEAD_SIZE), bf16),
            pltpu.VMEM((rows, heads, HEAD_SIZE), f32),
            pltpu.VMEM((rows, heads, HEAD_SIZE), f32),
            moved,
            levels,
            pltpu.VMEM((npre * slots, GROUP, HEAD_SIZE), bf16),
            pltpu.VMEM((npre * slots, GROUP, HEAD_SIZE), bf16),
            pltpu.VMEM((npre * slots, HEAD_SIZE), f32),
            pltpu.VMEM((npre * slots, HEAD_SIZE), f32),
            pltpu.VMEM((CORES, nx * rows, GROUP, HEAD_SIZE), bf16),
            pltpu.VMEM((CORES, nx * rows, HEAD_SIZE), f32),
            pltpu.VMEM((CORES, nx, rows, GROUP, HEAD_SIZE), bf16),
            pltpu.VMEM((CORES, nx, rows, HEAD_SIZE), f32),
            pltpu.VMEM((rows, heads, HEAD_SIZE), bf16),
            pltpu.VMEM((rows, width), bf16),
        ]
        + [dma] * 3
        + [dma((CORES,))] * 3
        + [dma((CORES,)), dma((CORES, nr))] * 2
        + [dma((CORES,))] * 2
        + [dma((rows,)), dma]
        + [dma((CORES,)), dma((CORES, npre * slots * GROUP // TILE + 1)), dma((CORES,))]
        + [dma((CORES,))] * 12
        + [dma],
        compiler_params=pltpu.CompilerParams(
            collective_id=0, has_side_effects=True, vmem_limit_bytes=60 * 1024 * 1024
        ),
    )(
        queries,
        prefix_ids[:, 0],
        suffix_lengths,
        prefix_keys[0],
        prefix_values[0],
        suffix_keys,
        suffix_values,
    )
    return out


def solution(mesh):
    in_specs = (
        P(("req", "pre"), None),
        P(("req", "pre"), None),
        P(("req", "pre")),
        P("pre", "req", None),
        P("pre", "req", None),
        P(("req", "pre"), None, None),
        P(("req", "pre"), None, None),
    )
    out_specs = P(("req", "pre"), None)
    return jax.shard_map(
        on_device, mesh=mesh, in_specs=in_specs, out_specs=out_specs, check_vma=False
    )
```

```python
import functools
import math

import jax
import jax.numpy as jnp
from jax import lax
from jax.experimental import pallas as pl
from jax.experimental.pallas import tpu as pltpu
from jax.sharding import PartitionSpec as P

HEAD_SIZE = 128
GROUP = 16
CAP = 2
CORES = 2
CHUNK = 256
TILE = 512
ALONG_Z = 4
MESH = pl.DeviceIdType.MESH
LOG2E = math.log2(math.e)
SCALE2 = HEAD_SIZE**-0.5 * LOG2E
NT = (((1,), (1,)), ((), ()))


def kernel(
    nr, npre, flat_ref, ids_ref, len_ref, pk_ref, pv_ref, sk_ref, sv_ref, out_ref,
    q_ref, meta, mrecv, msm, qx_a, qx_b, qo, qi, kb, vb, kt, acc, high, skv, so, sl, oo, lo, ob_a, ob_b, lb_a, lb_b, ox, lx, of, lf, outv,
    m_ss, m_rs, m_os, q_ss, q_rs, q_os, k_ss, k_rs, v_ss, v_rs, km_ss, vm_ss, s_s, sm_s,
    y_ss, y_rs, y_os, o_ss, o_rs, o_os, l_ss, l_rs, l_os, f_ss, f_rs, f_os, g_ss, g_rs, g_os,
):
    qx, ob, lb = (qx_a, qx_b), (ob_a, ob_b), (lb_a, lb_b)
    rows = flat_ref.shape[0]
    nx = nr // CORES
    slots = nx * CAP
    positions = kb.shape[2]
    heads = nr * GROUP
    tokens = skv.shape[2]
    r = lax.axis_index("req")
    p = lax.axis_index("pre")
    x = r // CORES
    core = lax.rem(r, CORES)
    mate = x * CORES + 1 - core

    tile = min(TILE, npre * slots * GROUP)
    sources = tile // (slots * GROUP)
    tiles = npre // sources
    tile_slots = sources * slots

    def block(index, size):
        return pl.ds(pl.multiple_of(index * size, size), size)

    def along(k):
        return lax.rem(x + k, nx)

    steps = [0, 1, nx - 1][:nx] + list(range(2, nx - 1))
    steps = list(dict.fromkeys(steps))

    def there(k):
        across = lax.rem(k, ALONG_Z)
        down = lax.rem(across + k // ALONG_Z, npre // ALONG_Z)
        return (
            lax.rem(p // ALONG_Z + down, npre // ALONG_Z) * ALONG_Z
            + lax.rem(lax.rem(p, ALONG_Z) + across, ALONG_Z)
        )

    def back(k):
        across = lax.rem(k, ALONG_Z)
        down = lax.rem(across + k // ALONG_Z, npre // ALONG_Z)
        return (
            lax.rem(p // ALONG_Z + npre // ALONG_Z - down, npre // ALONG_Z) * ALONG_Z
            + lax.rem(lax.rem(p, ALONG_Z) + ALONG_Z - across, ALONG_Z)
        )

    def suffix_copies(i):
        return (
            pltpu.make_async_copy(sk_ref.at[i], skv.at[i, 0], s_s.at[i]),
            pltpu.make_async_copy(sv_ref.at[i], skv.at[i, 1], s_s.at[i]),
        )

    def x_copy(which, h, src, dst, part=0):
        if which == "meta":
            return meta, mrecv.at[src], m_ss, m_rs, m_os
        if which == "query":
            head = dst * CORES + h
            return (
                q_ref.at[:, block(head, GROUP), :],
                qx[h].at[block(src, rows)],
                q_ss.at[h],
                q_rs.at[h],
                q_os.at[h],
            )
        if which == "key":
            return pk_ref.at[:, block(dst * CORES + h, HEAD_SIZE)], kb.at[h, part], k_ss.at[h], k_rs.at[h, part], k_rs.at[h, part]
        if which == "value":
            return (
                pv_ref.at[:, block(dst * CORES + h, HEAD_SIZE)],
                vb.at[h, part, :, pl.ds(0, HEAD_SIZE)],
                v_ss.at[h],
                v_rs.at[h, part],
                v_rs.at[h, part],
            )
        if which == "result":
            return ox.at[h, block(dst, rows)], of.at[h, src], f_ss.at[h], f_rs.at[h], f_os.at[h]
        return lx.at[h, block(dst, rows)], lf.at[h, src], g_ss.at[h], g_rs.at[h], g_os.at[h]

    def y_copy(which, h, k):
        at = block(k, slots)
        if which == "query":
            return qo.at[h, at], qi.at[h, at], y_ss.at[h], y_rs.at[h, k // sources], y_os.at[h], there(k)
        if which == "result":
            return oo.at[h, at], ob[h].at[at], o_ss.at[h], o_rs.at[h], o_os.at[h], back(k)
        return lo.at[h, at], lb[h].at[at], l_ss.at[h], l_rs.at[h], l_os.at[h], back(k)

    def x_remote(which, h, src, dst, part=0):
        a, b, c, d, _ = x_copy(which, h, src, dst, part)
        return pltpu.make_async_remote_copy(
            a, b, c, d, device_id=(dst * CORES + core, p), device_id_type=MESH
        )

    def y_remote(which, h, k):
        a, b, c, d, _, to = y_copy(which, h, k)
        return pltpu.make_async_remote_copy(a, b, c, d, device_id=(r, to), device_id_type=MESH)

    def sent(ref, sem):
        pltpu.make_async_remote_copy(
            ref, ref, sem, sem, device_id=(mate, p), device_id_type=MESH
        ).wait_send()

    def arrived(ref, sem):
        pltpu.make_async_remote_copy(
            ref, ref, sem, sem, device_id=(mate, p), device_id_type=MESH
        ).wait_recv()

    others = pl.ds(0, nx - 1)
    other_rows = pl.ds(0, (nx - 1) * rows)
    other_slots = pl.ds(slots, (npre - 1) * slots)

    def send_block(which, h, n):
        return x_remote(which, h, x, along(nx - steps[n]), CORES * n)

    def take_block(which, h, n):
        return x_remote(which, h, along(steps[n]), x, CORES * n)

    def x_own(which, h):
        a, b, _, _, d = x_copy(which, h, x, x)
        return pltpu.make_async_copy(a, b, d)

    def y_own(which, h):
        a, b, _, _, d, _ = y_copy(which, h, 0)
        return pltpu.make_async_copy(a, b, d)

    def mate_copy(which, h, n):
        mine, theirs = CORES * n, CORES * n + 1
        if which == "key":
            a, b = kb.at[h, mine], kb.at[h, theirs]
            first, c, d = pk_ref.at[:, block(x * CORES + h, HEAD_SIZE)], km_ss.at[h], k_rs.at[h, theirs]
        else:
            a, b = vb.at[h, mine, :, pl.ds(0, HEAD_SIZE)], vb.at[h, theirs, :, pl.ds(0, HEAD_SIZE)]
            first, c, d = pv_ref.at[:, block(x * CORES + h, HEAD_SIZE)], vm_ss.at[h], v_rs.at[h, theirs]
        return pltpu.make_async_remote_copy(
            first if n == 0 else a, b, c, d, device_id=(mate, p), device_id_type=MESH
        )

    barrier = pltpu.get_barrier_semaphore()
    pl.semaphore_signal(barrier, inc=1, device_id=(mate, p), device_id_type=MESH)
    for k in range(1, nx):
        pl.semaphore_signal(
            barrier, inc=1, device_id=(along(k) * CORES + core, p), device_id_type=MESH
        )
    for k in range(1, npre):
        pl.semaphore_signal(barrier, inc=1, device_id=(r, lax.rem(p + k, npre)), device_id_type=MESH)

    vb[:, :, :, HEAD_SIZE:] = jnp.ones((CORES, nr, positions, HEAD_SIZE), jnp.bfloat16)
    wide = GROUP * HEAD_SIZE
    for g in range(nr):
        q_ref[:, g * GROUP : (g + 1) * GROUP, :] = flat_ref[:, g * wide : (g + 1) * wide].reshape(
            rows, GROUP, HEAD_SIZE
        )
    for h in range(CORES):
        for which in ("query", "key", "value"):
            x_own(which, h).start()

    row = lax.broadcasted_iota(jnp.int32, (rows, HEAD_SIZE), 0)
    column = lax.broadcasted_iota(jnp.int32, (rows, HEAD_SIZE), 1)

    ids = jnp.zeros_like(row)
    other = jnp.zeros_like(row)
    for i in range(rows):
        ids = jnp.where(row == i, ids_ref[i], ids)
        other = jnp.where(column == i, ids_ref[i], other)

    def total(mask, values, axis):
        return jnp.sum(jnp.where(mask, values, 0), axis=axis, keepdims=True)

    named_before = (other == ids) & (column < row)
    rank = total(named_before, 1, 1)
    holders = total(ids * CAP + rank == column, row, 0)
    down = lax.rem(ids // ALONG_Z - p // ALONG_Z + npre, npre // ALONG_Z)
    across = lax.rem(lax.rem(ids, ALONG_Z) - lax.rem(p, ALONG_Z) + ALONG_Z, ALONG_Z)
    step = lax.rem(down - across + npre, npre // ALONG_Z) * ALONG_Z + across
    places = step * slots + x * CAP + jnp.minimum(rank, CAP - 1)
    places = total(column == npre * CAP + row, places, 0)
    meta[...] = jnp.broadcast_to(holders + places, meta.shape)
    x_own("meta", 0).start()

    lane = lax.broadcasted_iota(jnp.int32, (heads, tokens), 1)

    def suffix(i):
        pltpu.make_async_copy(skv.at[i], skv.at[i], s_s.at[i]).wait()
        queries = q_ref[i]
        scores = jnp.concatenate(
            [
                lax.dot_general(
                    queries[g * GROUP : (g + 1) * GROUP],
                    skv[i, 0, :, g * HEAD_SIZE : (g + 1) * HEAD_SIZE],
                    NT,
                    preferred_element_type=jnp.float32,
                )
                for g in range(nr)
            ],
            axis=0,
        )
        valid = lane < len_ref[i]
        scores = jnp.where(valid, scores * SCALE2, -jnp.inf)
        top = jnp.max(scores, axis=1, keepdims=True)
        weights = jnp.where(valid, jnp.exp2(scores - top), 0.0)
        den = jnp.sum(weights, axis=1, keepdims=True)
        cast = weights.astype(jnp.bfloat16)
        num = jnp.concatenate(
            [
                jnp.dot(
                    cast[g * GROUP : (g + 1) * GROUP],
                    skv[i, 1, :, g * HEAD_SIZE : (g + 1) * HEAD_SIZE],
                    preferred_element_type=jnp.float32,
                )
                for g in range(nr)
            ],
            axis=0,
        )
        so[i] = num / den
        sl[i] = jnp.broadcast_to(top + jnp.log2(den), (heads, HEAD_SIZE))

    pl.semaphore_wait(barrier, 1 + nx - 1 + npre - 1)
    for k in range(1, nx):
        x_remote("meta", 0, x, along(k)).start()
    for h in range(CORES):
        for k in range(1, nx):
            x_remote("query", h, x, along(k)).start()
    for h in range(CORES):
        for which in ("key", "value"):
            mate_copy(which, h, 0).start()
        for n in range(1, nx):
            for which in ("key", "value"):
                send_block(which, h, n).start()

    @pl.loop(0, rows)
    def _(i):
        for copy in suffix_copies(i):
            copy.start()

    early = rows * 5 // 8
    pl.loop(0, early)(suffix)

    x_own("meta", 0).wait()
    arrived(mrecv.at[others], m_rs)
    to_smem = pltpu.make_async_copy(mrecv, msm, sm_s)
    to_smem.start()
    to_smem.wait()

    for h in range(CORES):
        x_own("query", h).wait()
        arrived(qx[h].at[other_rows], q_rs.at[h])

        def place(k, h=h):
            dst = there(k)
            for src in range(nx):
                for rank in range(CAP):
                    row = src * rows + jnp.clip(msm[src, 0, dst * CAP + rank], 0, rows - 1)
                    qo[h, k * slots + src * CAP + rank] = qx[h][row]

        @pl.loop(1, npre)
        def _(k, h=h, place=place):
            place(k)
            y_remote("query", h, k).start()

        place(0)
        y_own("query", h).start()

    pl.loop(early, rows)(suffix)

    picks = lax.broadcasted_iota(jnp.int32, (tile_slots, GROUP, HEAD_SIZE), 1) == lax.broadcasted_iota(
        jnp.int32, (tile_slots, GROUP, HEAD_SIZE), 2
    )

    chunk = min(CHUNK, positions)

    def attend(h, t, some):
        span = block(t, tile_slots)
        hold = block(t, tile)
        scaled = qi[h, span].reshape(tile, HEAD_SIZE).astype(jnp.float32) * SCALE2
        upper = scaled.astype(jnp.bfloat16)
        lower = (scaled - upper.astype(jnp.float32)).astype(jnp.bfloat16)
        queries = jnp.concatenate([upper, lower], axis=1)
        if 0 in some:
            top = jnp.full((tile, 1), -jnp.inf, jnp.float32)
            both = jnp.zeros((tile, 2 * HEAD_SIZE), jnp.float32)
        else:
            top = jnp.max(high[hold, :], axis=1, keepdims=True)
            both = acc[hold, :]
        for part in range(CORES * some[0], CORES * (some[-1] + 1)):
            for at in range(0, positions, chunk):
                scores = jnp.dot(
                    queries, kt[h, part, :, at : at + chunk], preferred_element_type=jnp.float32
                )
                higher = jnp.maximum(top, jnp.max(scores, axis=1, keepdims=True))
                cast = jnp.exp2(scores - higher).astype(jnp.bfloat16)
                both = both * jnp.exp2(top - higher) + jnp.dot(
                    cast, vb[h, part, at : at + chunk, :], preferred_element_type=jnp.float32
                )
                top = higher
        if nx - 1 not in some:
            high[hold, :] = jnp.broadcast_to(top, (tile, HEAD_SIZE))
            acc[hold, :] = both
            return
        den = both[:, HEAD_SIZE:]
        result = both[:, :HEAD_SIZE] / den
        level = top + jnp.log2(den)
        oo[h, span] = result.astype(jnp.bfloat16).reshape(tile_slots, GROUP, HEAD_SIZE)
        lo[h, span] = jnp.sum(
            jnp.where(picks, level.reshape(tile_slots, GROUP, HEAD_SIZE), 0.0), axis=1
        )

    def relay(h, some):
        for n in some:
            for which in ("key", "value"):
                if n > 0:
                    take_block(which, h, n).wait_recv()
                    mate_copy(which, h, n).start()

    def ready(h, some):
        for n in some:
            for which in ("key", "value"):
                if n == 0:
                    x_own(which, h).wait()
                mate_copy(which, h, n).wait_recv()

        @pl.loop(CORES * some[0], CORES * (some[-1] + 1))
        def _(part):
            turned = kb[h, part].T
            kt[h, part, :HEAD_SIZE] = turned
            kt[h, part, HEAD_SIZE:] = turned

    def prefix(h, some, after=None, when=max(tiles - 2, 0), later=None):
        @pl.loop(0, tiles)
        def _(t):
            if 0 in some:

                @pl.when(t == 0)
                def _():
                    y_own("query", h).wait()

                    arrived(qi.at[h, pl.ds(slots, tile_slots - slots)], y_rs.at[h, 0])

                @pl.when(t > 0)
                def _():
                    arrived(qi.at[h, block(t, tile_slots)], y_rs.at[h, t])

            attend(h, t, some)
            if nx - 1 in some:

                @pl.when(t == 0)
                def _():
                    y_own("result", h).start()
                    y_own("level", h).start()

                for s in range(sources):
                    k = t * sources + s

                    @pl.when(k > 0)
                    def _():
                        y_remote("result", h, k).start()
                        y_remote("level", h, k).start()

            if after is not None:
                pl.when(t == when)(after)
            if later is not None:
                pl.when(t == max(tiles - 2, 0))(later)

    def give_back(h):
        for which in ("result", "level"):
            y_own(which, h).wait()
        arrived(ob[h].at[other_slots], o_rs.at[h])
        arrived(lb[h].at[other_slots], l_rs.at[h])

        def pick(dst):
            for i in range(rows):
                slot = jnp.clip(msm[dst, 0, npre * CAP + i], 0, npre * slots - 1)
                ox[h, dst * rows + i] = ob[h][slot]
                lx[h, pl.ds(dst * rows + i, 1), :] = lb[h][pl.ds(slot, 1), :]

        for k in range(1, nx):
            dst = along(k)
            pick(dst)
            x_remote("result", h, x, dst).start()
            x_remote("level", h, x, dst).start()
        pick(x)
        x_own("result", h).start()
        x_own("level", h).start()

    chosen = lax.broadcasted_iota(jnp.int32, (nx, GROUP, HEAD_SIZE), 1) == lax.broadcasted_iota(
        jnp.int32, (nx, GROUP, HEAD_SIZE), 2
    )

    def combine(h):
        for which in ("result", "level"):
            x_own(which, h).wait()
        arrived(of.at[h, others], f_rs.at[h])
        arrived(lf.at[h, others], g_rs.at[h])

        @pl.loop(0, rows)
        def _(i):
            spread = jnp.broadcast_to(lf[h, :, i, :][:, None, :], (nx, GROUP, HEAD_SIZE))
            levels = jnp.sum(jnp.where(chosen, spread, 0.0), axis=2, keepdims=True)
            for g in range(nx):
                mine = slice((g * CORES + h) * GROUP, (g * CORES + h + 1) * GROUP)
                first = jnp.broadcast_to(levels[g], (GROUP, HEAD_SIZE))
                second = sl[i, mine]
                top = jnp.maximum(first, second)
                first = jnp.exp2(first - top)
                second = jnp.exp2(second - top)
                outv[i, mine] = (
                    (of[h, g, i].astype(jnp.float32) * first + so[i, mine] * second)
                    / (first + second)
                ).astype(jnp.bfloat16)

        for g in range(h, nr, CORES):
            columns = pl.ds(g * wide, wide)
            out_ref[:, columns] = outv[:, g * GROUP : (g + 1) * GROUP, :].reshape(rows, wide)

    near, far = [0], list(range(1, nx))
    ready(0, near)
    prefix(0, near)
    relay(0, far)
    ready(0, far)
    prefix(0, far)
    ready(1, near)
    prefix(1, near, lambda: relay(1, far[:-1]), 0, lambda: relay(1, far[-1:]))
    ready(1, far)
    prefix(1, far, lambda: give_back(0), 0)

    sent(mrecv.at[others], m_ss)
    for h in range(CORES):
        sent(qx[h].at[other_rows], q_ss.at[h])
        sent(kb.at[h, others], k_ss.at[h])
        sent(vb.at[h, others, :, pl.ds(0, HEAD_SIZE)], v_ss.at[h])
        sent(kb.at[h, pl.ds(0, nx)], km_ss.at[h])
        sent(vb.at[h, pl.ds(0, nx), :, pl.ds(0, HEAD_SIZE)], vm_ss.at[h])
        sent(qo.at[h, other_slots], y_ss.at[h])
    combine(0)
    give_back(1)
    for h in range(CORES):
        sent(oo.at[h, other_slots], o_ss.at[h])
        sent(lo.at[h, other_slots], l_ss.at[h])
    combine(1)
    for h in range(CORES):
        sent(ox.at[h, other_rows], f_ss.at[h])
        sent(lx.at[h, other_rows], g_ss.at[h])


def on_device(
    queries, prefix_ids, suffix_lengths, prefix_keys, prefix_values, suffix_keys, suffix_values
):
    rows, width = queries.shape
    npre = lax.axis_size("pre")
    nr = lax.axis_size("req")
    nx = nr // CORES
    heads = nr * GROUP
    slots = nx * CAP
    positions = prefix_keys.shape[1]
    tokens = suffix_keys.shape[1]
    assert width == heads * HEAD_SIZE

    bf16, f32 = jnp.bfloat16, jnp.float32
    vmem = pl.BlockSpec(memory_space=pltpu.VMEM)
    smem = pl.BlockSpec(memory_space=pltpu.SMEM)
    hbm = pl.BlockSpec(memory_space=pl.ANY)
    dma = pltpu.SemaphoreType.DMA
    moved = pltpu.VMEM((CORES, npre * slots, GROUP, HEAD_SIZE), bf16)
    levels = pltpu.VMEM((CORES, npre * slots, HEAD_SIZE), f32)
    out = pl.pallas_call(
        functools.partial(kernel, nr, npre),
        out_shape=pltpu.VMEM((rows, width), bf16),
        in_specs=[vmem, smem, smem, hbm, hbm, hbm, hbm],
        out_specs=vmem,
        scratch_shapes=[
            pltpu.VMEM((rows, heads, HEAD_SIZE), bf16),
            pltpu.VMEM((8, 128), jnp.int32),
            pltpu.VMEM((nx, 8, 128), jnp.int32),
            pltpu.SMEM((nx, 8, 128), jnp.int32),
            pltpu.VMEM((nx * rows, GROUP, HEAD_SIZE), bf16),
            pltpu.VMEM((nx * rows, GROUP, HEAD_SIZE), bf16),
            moved,
            moved,
            pltpu.VMEM((CORES, nr, positions, HEAD_SIZE), bf16),
            pltpu.VMEM((CORES, nr, positions, 2 * HEAD_SIZE), bf16),
            pltpu.VMEM((CORES, nr, 2 * HEAD_SIZE, positions), bf16),
            pltpu.VMEM((npre * slots * GROUP, 2 * HEAD_SIZE), f32),
            pltpu.VMEM((npre * slots * GROUP, HEAD_SIZE), f32),
            pltpu.VMEM((rows, 2, tokens, nr * HEAD_SIZE), bf16),
            pltpu.VMEM((rows, heads, HEAD_SIZE), f32),
            pltpu.VMEM((rows, heads, HEAD_SIZE), f32),
            moved,
            levels,
            pltpu.VMEM((npre * slots, GROUP, HEAD_SIZE), bf16),
            pltpu.VMEM((npre * slots, GROUP, HEAD_SIZE), bf16),
            pltpu.VMEM((npre * slots, HEAD_SIZE), f32),
            pltpu.VMEM((npre * slots, HEAD_SIZE), f32),
            pltpu.VMEM((CORES, nx * rows, GROUP, HEAD_SIZE), bf16),
            pltpu.VMEM((CORES, nx * rows, HEAD_SIZE), f32),
            pltpu.VMEM((CORES, nx, rows, GROUP, HEAD_SIZE), bf16),
            pltpu.VMEM((CORES, nx, rows, HEAD_SIZE), f32),
            pltpu.VMEM((rows, heads, HEAD_SIZE), bf16),
        ]
        + [dma] * 3
        + [dma((CORES,))] * 3
        + [dma((CORES,)), dma((CORES, nr))] * 2
        + [dma((CORES,))] * 2
        + [dma((rows,)), dma]
        + [dma((CORES,)), dma((CORES, npre * slots * GROUP // TILE + 1)), dma((CORES,))]
        + [dma((CORES,))] * 12,
        compiler_params=pltpu.CompilerParams(
            collective_id=0, has_side_effects=True, vmem_limit_bytes=60 * 1024 * 1024
        ),
    )(
        queries,
        prefix_ids[:, 0],
        suffix_lengths,
        prefix_keys[0],
        prefix_values[0],
        suffix_keys,
        suffix_values,
    )
    return out


def solution(mesh):
    in_specs = (
        P(("req", "pre"), None),
        P(("req", "pre"), None),
        P(("req", "pre")),
        P("pre", "req", None),
        P("pre", "req", None),
        P(("req", "pre"), None, None),
        P(("req", "pre"), None, None),
    )
    out_specs = P(("req", "pre"), None)
    return jax.shard_map(
        on_device, mesh=mesh, in_specs=in_specs, out_specs=out_specs, check_vma=False
    )
```
